1024 devices in a mesh: prow: 128 (over x, z_hi, y, core), pcol: 8 (over z_lo).
Axes of the slice: x: 4, y: 4, z: 32 (z_hi: 4, z_lo: 8; z = z_hi * 8 + z_lo), core: 2. Of those that a mesh axis runs over, the one named last changes fastest.
Arguments:
- ainv_sep: bfloat16 [128, 8, 24, 24576], P(None, 'pcol', None, 'prow'), may hold values from -6 to 6
- lower_blocks: bfloat16 [24576, 768], P(('prow', 'pcol')), may hold values from -0.0546875 to 0.0546875
- pattern: int32 [1024, 12], replicated, may hold values from 0 to 1, as said below
- diag_inv: float32 [768, 64], replicated, may hold values from -6 to 6
Outputs:
- offdiag: float32 [24576, 768], P(('prow', 'pcol'))
- diagonal: float32 [768, 64], replicated
The draws below stay inside these ranges and needn't reach their ends.
Inputs may be any that keep to these rules, and one draw needn't show every extreme that they name: `pattern`: each block row meets between (3) and 6 supernodes, and some block row meets exactly 6.
All inputs are finite; a program needn't handle non-finite values.
Results may differ from the reference program's by a relative error of at most 0.0003.
Values may be sent and summed in bfloat16 or wider, within the bound.
A program may use at most 64 MiB of HBM per device.

```python
import jax
import jax.numpy as jnp
from jax import lax

W = 64
KS = 12
RB = 24
KL = 6
NS = 24576
NK = 768
N_PROW = 128
N_PCOL = 8
DEVICES = 1024


def draw_pattern(key, part):
    key = jax.random.fold_in(key, 11)
    first, second, third = jax.random.split(key, 3)
    lowest = max(1, (KL + 1) // 2)
    counts = jax.random.randint(first, (DEVICES,), lowest, KL + 1)
    full_row = jax.random.randint(second, (), 0, DEVICES)
    counts = jnp.where(jnp.arange(DEVICES) == full_row, KL, counts)
    scores = jax.random.randint(third, (DEVICES, KS), 0, 1 << 20) * KS + jnp.arange(KS)[None, :]
    ranks = jnp.argsort(jnp.argsort(scores, axis=1), axis=1)
    return (ranks < counts[:, None]).astype(jnp.int32)


def block_levels(rng, dims, shards, least, largest):
    loudness, own = 1.0, jax.random.fold_in(rng, 6)
    for dim, parts in shards:
        heights = jnp.exp(jax.random.uniform(jax.random.fold_in(own, dim), (parts,), jnp.float32, least / len(shards), largest / len(shards)))
        loudness = loudness * jnp.repeat(heights, dims[dim] // parts).reshape([-1 if axis == dim else 1 for axis in range(len(dims))])
    return loudness


def noise(key, shape, scale, bound, shards=(), held_as=jnp.bfloat16):
    loudness = block_levels(key, shape, shards, -0.22, 0.18) if shards else 1.0
    entries = jax.random.normal(key, shape, jnp.float32) * scale * loudness
    return jnp.minimum(jnp.maximum(entries, -bound), bound).astype(held_as)


def setup_inputs(seed: int = 0) -> dict:
    seeds = jax.random.split(jax.random.key(seed), 5)
    ainv_sep = noise(seeds[0], (N_PROW, N_PCOL, RB, NS), 1.0, 6.0, ((1, 8), (3, 128)))
    lower_blocks = noise(seeds[1], (NS, NK), (NS // 2) ** -0.5, 0.0546875, ((0, 1024),))
    pattern = draw_pattern(jax.random.fold_in(seeds[4], 71), 0)
    diag_inv = noise(seeds[3], (NK, W), 1.0, 6.0, (), jnp.float32)
    return {"ainv_sep": ainv_sep, "lower_blocks": lower_blocks, "pattern": pattern, "diag_inv": diag_inv}


def reference(ainv_sep, lower_blocks, pattern, diag_inv):
    sep_matrix = ainv_sep.reshape(NS, NS)
    live = jnp.repeat(jnp.repeat(pattern, RB, axis=0), W, axis=1)
    masked = jnp.where(live != 0, lower_blocks, jnp.zeros_like(lower_blocks))
    offdiag = -lax.dot_general(sep_matrix, masked, (((0,), (0,)), ((), ())), preferred_element_type=jnp.float32)
    lower_three = masked.astype(jnp.float32).reshape(NS, KS, W)
    image_three = offdiag.reshape(NS, KS, W)
    correction = jnp.einsum("iks,ikt->kst", lower_three, image_three, precision=lax.Precision.HIGHEST)
    diagonal = diag_inv - correction.reshape(NK, W)
    return offdiag, diagonal
```

```python
import functools

import jax
import jax.numpy as jnp
from jax import lax
from jax.experimental import pallas as pl
from jax.experimental.pallas import tpu as pltpu
from jax.sharding import PartitionSpec as P

MESH = pl.DeviceIdType.MESH
F32, BF16 = jnp.float32, jnp.bfloat16
GROUPS = [[j for j in range(3) if (j <= m if m < 3 else j >= m - 3)] for m in range(6)]


def tile(m):
    return slice(m * 128, (m + 1) * 128)


def prow_of(x, zh, y, c):
    return ((x * 4 + zh) * 4 + y) * 2 + c


def place(i):
    c, a, w, zh = i // 64, (i // 16) % 4, (i // 4) % 4, i % 4
    x = a * (1 - c) + w * c
    y = w * (1 - c) + a * c
    return prow_of(x, zh, y, c)


def slot_rows(pat):
    rows = [pat[k : k + 1, :] for k in range(12)]
    out = [None] * 12
    run = jnp.zeros_like(rows[0])
    for k in range(6):
        run = run + rows[k]
        out[k] = run * rows[k]
    run = jnp.full_like(rows[0], 6.0)
    for k in range(11, 5, -1):
        out[k] = run * rows[k]
        run = run - rows[k]
    return jnp.concatenate(out + [jnp.zeros_like(rows[0])] * 4, axis=0)


def kernel(
    pat_ref, low_ref, dinv_ref, g_ref, off_ref, diag_ref,
    cb, dd, cp, gv, gt, tm, tp, ee, mp, pt, rr, rl, sh, b1, b2, b3, b4, b5, b6,
    gsem, sa, ra, sb, rb, sc, rc, sd, rd, sp, rp, s_r, r_r, s_l, r_l,
    s1, r1, s2, r2, s3, r3, s4, r4, s5, r5, s6, r6,
):
    p = lax.axis_index("prow")
    zl = lax.axis_index("pcol")
    c, y, zh, x = p % 2, (p // 2) % 4, (p // 8) % 4, p // 32
    w = y * (1 - c) + x * c
    a = x * (1 - c) + y * c

    def send(src, dst, ssem, rsem, prow, pcol):
        return pltpu.make_async_remote_copy(
            src_ref=src, dst_ref=dst, send_sem=ssem, recv_sem=rsem,
            device_id=(prow, pcol), device_id_type=MESH,
        )

    def at_zh(k):
        return prow_of(x, (zh + k) % 4, y, c)

    def at_x(k):
        return prow_of((x + k) % 4, zh, y, c)

    def at_w(k):
        v = (w + k) % 4
        return prow_of(x * (1 - c) + v * c, zh, v * (1 - c) + y * c, c)

    def at_a(k):
        v = (a + k) % 4
        return prow_of(v * (1 - c) + x * c, zh, y * (1 - c) + v * c, c)

    core_peer = prow_of(x, zh, y, 1 - c)
    me8 = y * 2 + c

    def at_8(k):
        v = (me8 + k) % 8
        return prow_of(x, zh, v // 2, v % 2)

    g_copy = pltpu.make_async_copy(g_ref, gv, gsem)
    g_copy.start()

    barrier = pltpu.get_barrier_semaphore()
    for k in range(1, 4):
        pl.semaphore_signal(barrier, inc=1, device_id=(at_zh(k), zl), device_id_type=MESH)
        pl.semaphore_signal(barrier, inc=1, device_id=(at_x(k), zl), device_id_type=MESH)
    for k in range(1, 8):
        pl.semaphore_signal(barrier, inc=1, device_id=(at_8(k), zl), device_id_type=MESH)
        pl.semaphore_signal(barrier, inc=1, device_id=(p, (zl + k) % 8), device_id_type=MESH)

    slots = slot_rows(pat_ref[...].astype(F32)).astype(BF16)
    row = lax.broadcasted_iota(jnp.int32, (144, 1024), 0)
    lane = lax.broadcasted_iota(jnp.int32, (144, 1024), 1)
    wanted = jnp.where(row < 128, place(row % 128) * 8 + zl, p * 8 + row % 8)
    pick = jnp.where(lane == wanted, 1.0, 0.0).astype(BF16)
    table = lax.dot_general(pick, slots, (((1,), (1,)), ((), ())), preferred_element_type=F32)
    low_half = lax.broadcasted_iota(jnp.int32, (144, 128), 1) < 64
    for m in range(6):
        t = jnp.where(low_half, table[:, 2 * m : 2 * m + 1], table[:, 2 * m + 1 : 2 * m + 2])
        tm[:, tile(m)] = t[:128].astype(BF16)
        for q in range(8):
            tp[q, :, tile(m)] = t[128 + q : 129 + q]

    half24 = lax.broadcasted_iota(jnp.int32, (24, 128), 1) < 64
    own = cb.at[w * 4 + zh]
    mine = tp[zl]
    parts = [None] * 3
    for m in range(6):
        val = low_ref[:, tile(m)].astype(F32)
        t = jnp.broadcast_to(mine[:, tile(m)], (24, 128))
        val_r, t_r = pltpu.roll(val, 64, 1), pltpu.roll(t, 64, 1)
        for j in GROUPS[m]:
            goal = jnp.where(half24, 2.0 * j + 1.0, 2.0 * j + 2.0)
            got = jnp.where(t == goal, val, 0.0) + jnp.where(t_r == goal, val_r, 0.0)
            parts[j] = got if parts[j] is None else parts[j] + got
    for j in range(3):
        own[:, tile(j)] = parts[j].astype(BF16)
        cp[zl, :, tile(j)] = parts[j].astype(BF16)

    pl.semaphore_wait(barrier, 20)

    to_zh = [send(own, own, sa.at[k - 1], ra.at[zh], at_zh(k), zl) for k in range(1, 4)]
    for copy in to_zh:
        copy.start()

    def forward(v):
        ref = cb.at[w * 4 + v]
        return [send(ref, ref, sb.at[v, k - 1], rb.at[w * 4 + v], at_w(k), zl) for k in range(1, 4)]

    for copy in forward(zh):
        copy.start()

    gi = lax.broadcasted_iota(jnp.int32, (128, 128), 0)
    gj = lax.broadcasted_iota(jnp.int32, (128, 128), 1)
    perm = jnp.where(gi == place(gj), -1.0, 0.0).astype(BF16)
    oi = lax.broadcasted_iota(jnp.int32, (384, 384), 0)
    oj = lax.broadcasted_iota(jnp.int32, (384, 384), 1)
    order = jnp.where(oj == (oi % 16) * 24 + oi // 16, 1.0, 0.0).astype(BF16)

    for k in (1, 3, 2):
        v = (zh + k) % 4
        ref = cb.at[w * 4 + v]
        send(ref, ref, sa.at[k - 1], ra.at[v], at_zh(k), zl).wait_recv()
        for copy in forward(v):
            copy.start()

    to_zl = [
        send(cp.at[zl], cp.at[zl], sp.at[k], rp.at[zl], p, (zl + k) % 8) for k in range(1, 8)
    ]
    for copy in to_zl:
        copy.start()

    g_copy.wait()

    @pl.loop(0, 24)
    def _(r):
        gt[:, pl.ds(pl.multiple_of(r * 128, 128), 128)] = jnp.dot(
            gv[r], perm, preferred_element_type=F32
        ).astype(BF16)

    for k in (1, 3, 2):
        for v in range(4):
            slot = ((w + k) % 4) * 4 + v
            ref = cb.at[slot]
            send(ref, ref, sb.at[v, k - 1], rb.at[slot], at_w(k), zl).wait_recv()

    group = cb[...].astype(F32).reshape(384, 384).astype(BF16)
    group = jnp.dot(order, group, preferred_element_type=F32)
    dd[c * 4 + a] = group.reshape(24, 16, 384).astype(BF16)

    mine_d = dd.at[c * 4 + a]
    to_a = [send(mine_d, mine_d, sc.at[k - 1], rc.at[a], at_a(k), zl) for k in range(1, 4)]
    for copy in to_a:
        copy.start()

    def to_core(v):
        ref = dd.at[c * 4 + v]
        return send(ref, ref, sd.at[v], rd.at[v], core_peer, zl)

    to_core(a).start()

    half16 = lax.broadcasted_iota(jnp.int32, (16, 128), 1) < 64
    plain = [jnp.where(half16, 2.0 * j + 1.0, 2.0 * j + 2.0).astype(BF16) for j in range(3)]
    swapped = [jnp.where(half16, 2.0 * j + 2.0, 2.0 * j + 1.0).astype(BF16) for j in range(3)]

    def expand(g):
        start = pl.multiple_of(g * 16, 16)

        @pl.loop(0, 24)
        def _(r):
            val = [dd[g, r, :, tile(j)] for j in range(3)]
            val_r = [pltpu.roll(v.astype(F32), 64, 1).astype(BF16) for v in val]
            for m in range(6):
                t = tm[pl.ds(start, 16), tile(m)]
                acc = jnp.zeros((16, 128), BF16)
                for j in GROUPS[m]:
                    acc = jnp.where(t == plain[j], val[j], acc)
                    acc = jnp.where(t == swapped[j], val_r[j], acc)
                ee[pl.ds(pl.multiple_of(r * 128 + g * 16, 16), 16), tile(m)] = acc

    expand(c * 4 + a)

    for k in range(1, 8):
        v = (zl + k) % 8
        send(cp.at[v], cp.at[v], sp.at[k], rp.at[v], p, v).wait_recv()
    goal_p = [jnp.where(half24, 2.0 * j + 1.0, 2.0 * j + 2.0) for j in range(3)]
    goal_s = [jnp.where(half24, 2.0 * j + 2.0, 2.0 * j + 1.0) for j in range(3)]

    @pl.loop(0, 8)
    def _(q):
        val = [cp[q, :, tile(j)].astype(F32) for j in range(3)]
        val_r = [pltpu.roll(v, 64, 1) for v in val]
        for m in range(6):
            t = jnp.broadcast_to(tp[q, :, tile(m)], (24, 128))
            acc = jnp.zeros((24, 128), F32)
            for j in GROUPS[m]:
                acc = jnp.where(t == goal_p[j], val[j], acc)
                acc = jnp.where(t == goal_s[j], val_r[j], acc)
            mp[q, :, tile(m)] = acc

    other = y * (1 - c) + x * c

    def from_core(v):
        ref = dd.at[(1 - c) * 4 + v]
        send(ref, ref, sd.at[v], rd.at[v], core_peer, zl).wait_recv()
        expand((1 - c) * 4 + v)

    from_core(other)
    for k in (1, 3, 2):
        v = (a + k) % 4
        ref = dd.at[c * 4 + v]
        send(ref, ref, sc.at[k - 1], rc.at[v], at_a(k), zl).wait_recv()
        to_core(v).start()
        expand(c * 4 + v)
    for k in (1, 3, 2):
        from_core((other + k) % 4)

    @pl.loop(0, 3)
    def _(n):
        cols = pl.ds(pl.multiple_of(n * 256, 256), 256)
        got = jnp.dot(gt[...], ee[:, cols], preferred_element_type=F32)
        pt[:, :, cols] = got.reshape(8, 24, 256)

    def step_right(j):
        @pl.when(j > zl)
        def _():
            copy = send(rr.at[j], rr.at[j], s_r.at[j], r_r.at[j], p, (zl + 1) % 8)

            @pl.when(zl > 0)
            def _():
                copy.wait_recv()
                rr[j] = rr[j] + pt[j]

            @pl.when(zl == 0)
            def _():
                rr[j] = pt[j]

            if j <= 5:
                nxt = j + 2
                send(rr.at[nxt], rr.at[nxt], s_r.at[nxt], r_r.at[nxt], p, (zl + 1) % 8).wait_send()
            copy.start()

    def step_left(j):
        @pl.when(j < zl)
        def _():
            copy = send(rl.at[j], rl.at[j], s_l.at[j], r_l.at[j], p, (zl + 7) % 8)

            @pl.when(zl < 7)
            def _():
                copy.wait_recv()
                rl[j] = rl[j] + pt[j]

            @pl.when(zl == 7)
            def _():
                rl[j] = pt[j]

            if j >= 2:
                nxt = j - 2
                send(rl.at[nxt], rl.at[nxt], s_l.at[nxt], r_l.at[nxt], p, (zl + 7) % 8).wait_send()
            copy.start()

    step_right(7)
    step_left(0)

    half64 = lax.broadcasted_iota(jnp.int32, (64, 128), 1) < 64
    for m in range(6):
        part = pt[:, :, tile(m)].reshape(192, 128)
        fac = mp[:, :, tile(m)].reshape(192, 128).astype(BF16)
        hi = part.astype(BF16)
        lo = (part - hi.astype(F32)).astype(BF16)
        dims = (((0,), (0,)), ((), ()))
        both = lax.dot_general(hi, fac, dims, preferred_element_type=F32)
        both = both + lax.dot_general(lo, fac, dims, preferred_element_type=F32)
        sh[:, :, tile(m)] = jnp.where(half64, both[:64], both[64:]).reshape(8, 8, 128)

    b1[me8] = sh[me8]
    to_1 = []
    for k in range(1, 8):
        v = (me8 + k) % 8
        to_1.append(send(sh.at[v], b1.at[me8], s1.at[k], r1.at[me8], at_8(k), zl))
    for copy in to_1:
        copy.start()

    def phase1():
        for k in range(1, 8):
            v = (me8 + k) % 8
            send(sh.at[v], b1.at[v], s1.at[k], r1.at[v], at_8(k), zl).wait_recv()
        b2[x] = functools.reduce(lambda u, v: u + v, [b1[v] for v in range(8)])
        for k in range(1, 4):
            send(b2.at[x], b2.at[x], s2.at[k], r2.at[x], at_x(k), zl).start()

    xx = x - x // 3
    cols = pl.ds(pl.multiple_of(xx * 256, 256), 256)

    def phase2():
        for k in range(1, 4):
            v = (x + k) % 4
            send(b2.at[v], b2.at[v], s2.at[k], r2.at[v], at_x(k), zl).wait_recv()
        b3[zl] = functools.reduce(lambda u, v: u + v, [b2[v, :, cols] for v in range(4)])
        for k in range(1, 8):
            send(b3.at[zl], b3.at[zl], s3.at[k], r3.at[zl], p, (zl + k) % 8).start()

    def phase3():
        for k in range(1, 8):
            v = (zl + k) % 8
            send(b3.at[v], b3.at[v], s3.at[k], r3.at[v], p, v).wait_recv()
        b4[zh] = functools.reduce(lambda u, v: u + v, [b3[v] for v in range(8)])
        for k in range(1, 4):
            send(b4.at[zh], b4.at[zh], s4.at[k], r4.at[zh], at_zh(k), zl).start()

    def phase4():
        for k in range(1, 4):
            v = (zh + k) % 4
            send(b4.at[v], b4.at[v], s4.at[k], r4.at[v], at_zh(k), zl).wait_recv()
        b5[x] = functools.reduce(lambda u, v: u + v, [b4[v] for v in range(4)])
        for k in range(1, 4):
            send(b5.at[x], b5.at[x], s5.at[k], r5.at[x], at_x(k), zl).start()

    def phase5():
        for k in range(1, 4):
            v = (x + k) % 4
            send(b5.at[v], b5.at[v], s5.at[k], r5.at[v], at_x(k), zl).wait_recv()
        for v in range(3):
            b6[me8, :, v * 256 : (v + 1) * 256] = b5[v]
        for k in range(1, 8):
            send(b6.at[me8], b6.at[me8], s6.at[k], r6.at[me8], at_8(k), zl).start()

    def phase6():
        for k in range(1, 8):
            v = (me8 + k) % 8
            send(b6.at[v], b6.at[v], s6.at[k], r6.at[v], at_8(k), zl).wait_recv()
        diag_ref[...] = dinv_ref[...] - b6[...].reshape(64, 768)

    phases = [phase1, phase2, phase3, phase4, phase5, phase6]
    for t in range(1, 7):
        step_right(7 - t)
        step_left(t)

    off_ref[...] = pt[zl]

    @pl.when(zl > 0)
    def _():
        send(rr.at[zl], rr.at[zl], s_r.at[zl], r_r.at[zl], p, (zl + 1) % 8).wait_recv()
        off_ref[...] += rr[zl]

    @pl.when(zl < 7)
    def _():
        send(rl.at[zl], rl.at[zl], s_l.at[zl], r_l.at[zl], p, (zl + 7) % 8).wait_recv()
        off_ref[...] += rl[zl]

    for phase in phases:
        phase()

    for copy in to_zh + to_zl + to_a + to_1:
        copy.wait_send()
    for v in range(4):
        for copy in forward(v):
            copy.wait_send()
        to_core(v).wait_send()
    for j in range(1, 8):

        @pl.when(jnp.logical_and(j > zl, j <= zl + 2))
        def _():
            send(rr.at[j], rr.at[j], s_r.at[j], r_r.at[j], p, (zl + 1) % 8).wait_send()

    for j in range(7):

        @pl.when(jnp.logical_and(j < zl, j >= zl - 2))
        def _():
            send(rl.at[j], rl.at[j], s_l.at[j], r_l.at[j], p, (zl + 7) % 8).wait_send()

    for k in range(1, 4):
        send(b2.at[x], b2.at[x], s2.at[k], r2.at[x], at_x(k), zl).wait_send()
        send(b4.at[zh], b4.at[zh], s4.at[k], r4.at[zh], at_zh(k), zl).wait_send()
        send(b5.at[x], b5.at[x], s5.at[k], r5.at[x], at_x(k), zl).wait_send()
    for k in range(1, 8):
        send(b3.at[zl], b3.at[zl], s3.at[k], r3.at[zl], p, (zl + k) % 8).wait_send()
        send(b6.at[me8], b6.at[me8], s6.at[k], r6.at[me8], at_8(k), zl).wait_send()


def body(ainv_sep, lower_blocks, pattern, diag_inv):
    dma = pltpu.SemaphoreType.DMA
    vmem = pltpu.VMEM
    off, diag = pl.pallas_call(
        kernel,
        out_shape=(
            jax.ShapeDtypeStruct((24, 768), F32),
            jax.ShapeDtypeStruct((64, 768), F32),
        ),
        in_specs=[pl.BlockSpec(memory_space=vmem)] * 3 + [pl.BlockSpec(memory_space=pl.ANY)],
        out_specs=(pl.BlockSpec(memory_space=vmem), pl.BlockSpec(memory_space=vmem)),
        scratch_shapes=[
            vmem((16, 24, 384), BF16),
            vmem((8, 24, 16, 384), BF16),
            vmem((8, 24, 384), BF16),
            vmem((24, 192, 128), BF16),
            vmem((192, 3072), BF16),
            vmem((128, 768), BF16),
            vmem((8, 1, 768), F32),
            vmem((3072, 768), BF16),
            vmem((8, 24, 768), F32),
            vmem((8, 24, 768), F32),
            vmem((8, 24, 768), F32),
            vmem((8, 24, 768), F32),
            vmem((8, 8, 768), F32),
            vmem((8, 8, 768), F32),
            vmem((4, 8, 768), F32),
            vmem((8, 8, 256), F32),
            vmem((4, 8, 256), F32),
            vmem((4, 8, 256), F32),
            vmem((8, 8, 768), F32),
            dma,
            dma((3,)), dma((4,)),
            dma((4, 3)), dma((16,)),
            dma((3,)), dma((4,)),
            dma((4,)), dma((4,)),
            dma((8,)), dma((8,)),
            dma((8,)), dma((8,)),
            dma((8,)), dma((8,)),
            dma((8,)), dma((8,)),
            dma((4,)), dma((4,)),
            dma((8,)), dma((8,)),
            dma((4,)), dma((4,)),
            dma((4,)), dma((4,)),
            dma((8,)), dma((8,)),
        ],
        compiler_params=pltpu.CompilerParams(
            collective_id=0, has_side_effects=True, vmem_limit_bytes=48 * 1024 * 1024
        ),
    )(
        pattern.T,
        lower_blocks,
        diag_inv.T,
        ainv_sep.transpose(1, 2, 3, 0).reshape(24, 192, 128),
    )
    return off, diag.T


def solution(mesh):
    return jax.shard_map(
        body,
        mesh=mesh,
        in_specs=(P(None, "pcol", None, "prow"), P(("prow", "pcol"), None), P(), P()),
        out_specs=(P(("prow", "pcol"), None), P()),
        check_vma=False,
    )
```

```python
import functools

import jax
import jax.numpy as jnp
from jax import lax
from jax.experimental import pallas as pl
from jax.experimental.pallas import tpu as pltpu
from jax.sharding import PartitionSpec as P

MESH = pl.DeviceIdType.MESH
F32, BF16 = jnp.float32, jnp.bfloat16
GROUPS = [[j for j in range(3) if (j <= m if m < 3 else j >= m - 3)] for m in range(6)]


def tile(m):
    return slice(m * 128, (m + 1) * 128)


def prow_of(x, zh, y, c):
    return ((x * 4 + zh) * 4 + y) * 2 + c


def place(i):
    c, a, w, zh = i >> 6, (i >> 4) & 3, (i >> 2) & 3, i & 3
    x = jnp.where(c == 0, a, w)
    y = jnp.where(c == 0, w, a)
    return (x << 5) + (zh << 3) + (y << 1) + c


def slot_rows(pat):
    rows = [pat[k : k + 1, :] for k in range(12)]
    out = [None] * 12
    run = jnp.zeros_like(rows[0])
    for k in range(6):
        run = run + rows[k]
        out[k] = run * rows[k]
    run = jnp.full_like(rows[0], 6.0)
    for k in range(11, 5, -1):
        out[k] = run * rows[k]
        run = run - rows[k]
    return jnp.concatenate(out + [jnp.zeros_like(rows[0])] * 4, axis=0)


def kernel(
    pat_hbm, low_hbm, dinv_hbm, g_hbm, off_ref, diag_ref,
    pat_ref, low_ref, dinv_ref, cb, dd, cp, gv, gt, tm, tp, ee, mp, ft, pt, rr, rl, sh, b1, b3, b4, b6,
    isem, sa, ra, sb, rb, sc, rc, sd, rd, sp, rp, s_r, r_r, s_l, r_l,
    s1, r1, s3, r3, s4, r4, s6, r6,
):
    p = lax.axis_index("prow")
    zl = lax.axis_index("pcol")
    c, y, zh, x = p % 2, (p // 2) % 4, (p // 8) % 4, p // 32
    w = y * (1 - c) + x * c
    a = x * (1 - c) + y * c

    def send(src, dst, ssem, rsem, prow, pcol):
        return pltpu.make_async_remote_copy(
            src_ref=src, dst_ref=dst, send_sem=ssem, recv_sem=rsem,
            device_id=(prow, pcol), device_id_type=MESH,
        )

    def at_zh(k):
        return prow_of(x, (zh + k) % 4, y, c)

    def at_w(k):
        v = (w + k) % 4
        return prow_of(x * (1 - c) + v * c, zh, v * (1 - c) + y * c, c)

    def at_a(k):
        v = (a + k) % 4
        return prow_of(v * (1 - c) + x * c, zh, y * (1 - c) + v * c, c)

    core_peer = prow_of(x, zh, y, 1 - c)
    d = (x * 4 + y) * 2 + c

    def in_plane(v):
        return prow_of((v // 8) % 4, zh, (v // 2) % 4, v % 2)


    barrier = pltpu.get_barrier_semaphore()
    for k in (1, 3):
        pl.semaphore_signal(barrier, inc=1, device_id=(at_zh(k), zl), device_id_type=MESH)
    for k in range(1, 8):
        pl.semaphore_signal(barrier, inc=1, device_id=(p, (zl + k) % 8), device_id_type=MESH)
    for k in range(1, 32):
        pl.semaphore_signal(barrier, inc=1, device_id=(in_plane(d + k), zl), device_id_type=MESH)

    pairs = [(pat_hbm, pat_ref), (low_hbm, low_ref), (g_hbm, gv), (dinv_hbm, dinv_ref)]
    loads = [pltpu.make_async_copy(u, v, isem.at[k]) for k, (u, v) in enumerate(pairs)]
    for copy in loads:
        copy.start()
    loads[0].wait()
    loads[1].wait()

    slots = slot_rows(pat_ref[...].astype(F32)).astype(BF16)
    row = lax.broadcasted_iota(jnp.int32, (144, 128), 0)
    lane = lax.broadcasted_iota(jnp.int32, (144, 128), 1)
    wanted = jnp.where(row < 128, (place(row & 127) << 3) + zl, p * 8 + (row & 7)) - lane
    pick = [jnp.where(wanted == 128 * k, 1.0, 0.0).astype(BF16) for k in range(8)]
    pick = jnp.concatenate(pick, axis=1)
    table = lax.dot_general(pick, slots, (((1,), (1,)), ((), ())), preferred_element_type=F32)
    low_half = lane < 64
    for m in range(6):
        t = jnp.where(low_half, table[:, 2 * m : 2 * m + 1], table[:, 2 * m + 1 : 2 * m + 2])
        tm[:, tile(m)] = t[:128].astype(BF16)
        for q in range(8):
            tp[q, :, tile(m)] = t[128 + q : 129 + q]

    half24 = lax.broadcasted_iota(jnp.int32, (24, 128), 1) < 64
    own = cb.at[w * 4 + zh]
    mine = tp[zl]
    parts = [None] * 3
    for m in range(6):
        val = low_ref[:, tile(m)].astype(F32)
        t = jnp.broadcast_to(mine[:, tile(m)], (24, 128))
        val_r, t_r = pltpu.roll(val, 64, 1), pltpu.roll(t, 64, 1)
        for j in GROUPS[m]:
            goal = jnp.where(half24, 2.0 * j + 1.0, 2.0 * j + 2.0)
            got = jnp.where(t == goal, val, 0.0) + jnp.where(t_r == goal, val_r, 0.0)
            parts[j] = got if parts[j] is None else parts[j] + got
    for j in range(3):
        own[:, tile(j)] = parts[j].astype(BF16)
        cp[zl, :, tile(j)] = parts[j].astype(BF16)

    pl.semaphore_wait(barrier, 40)

    to_zh = [send(own, own, sa.at[k // 2], ra.at[zh], at_zh(k), zl) for k in (1, 3)]
    for copy in to_zh:
        copy.start()

    def forward(v):
        ref = cb.at[w * 4 + v]
        return [send(ref, ref, sb.at[v, k - 1], rb.at[w * 4 + v], at_w(k), zl) for k in range(1, 4)]

    for copy in forward(zh):
        copy.start()

    gi = lax.broadcasted_iota(jnp.int32, (128, 128), 0)
    gj = lax.broadcasted_iota(jnp.int32, (128, 128), 1)
    perm = jnp.where(gi == place(gj), -1.0, 0.0).astype(BF16)
    oi = lax.broadcasted_iota(jnp.int32, (384, 128), 0)
    oj = lax.broadcasted_iota(jnp.int32, (384, 128), 1)
    source = (oi & 15) * 24 + (oi >> 4) - oj
    order = [jnp.where(source == 128 * k, 1.0, 0.0).astype(BF16) for k in range(3)]
    order = jnp.concatenate(order, axis=1)

    loads[2].wait()
    loads[3].wait()
    for r in range(24):
        gt[:, tile(r)] = jnp.dot(gv[r], perm, preferred_element_type=F32).astype(BF16)

    for k in (3 - 2 * c, 1 + 2 * c, 2):
        v = (zh + k) % 4
        ref = cb.at[w * 4 + v]
        send(ref, ref, sa.at[2], ra.at[v], at_zh(1 + 2 * c), zl).wait_recv()
        if len(to_zh) == 2:
            to_zh.append(send(ref, ref, sa.at[2], ra.at[v], at_zh(1 + 2 * c), zl))
            to_zh[2].start()
        for copy in forward(v):
            copy.start()

    to_zl = [
        send(cp.at[zl], cp.at[zl], sp.at[k], rp.at[zl], p, (zl + k) % 8) for k in range(1, 8)
    ]
    for copy in to_zl:
        copy.start()

    for k in (1, 3, 2):
        for v in range(4):
            slot = ((w + k) % 4) * 4 + v
            ref = cb.at[slot]
            send(ref, ref, sb.at[v, k - 1], rb.at[slot], at_w(k), zl).wait_recv()

    group = cb[...].astype(F32).reshape(384, 384).astype(BF16)
    group = jnp.dot(order, group, preferred_element_type=F32)
    dd[c * 4 + a] = group.reshape(24, 16, 384).astype(BF16)

    mine_d = dd.at[c * 4 + a]
    to_a = [send(mine_d, mine_d, sc.at[k - 1], rc.at[a], at_a(k), zl) for k in range(1, 4)]
    for copy in to_a:
        copy.start()

    def to_core(v):
        ref = dd.at[c * 4 + v]
        return send(ref, ref, sd.at[v], rd.at[v], core_peer, zl)

    to_core(a).start()

    half16 = lax.broadcasted_iota(jnp.int32, (16, 128), 1) < 64
    plain = [jnp.where(half16, 2.0 * j + 1.0, 2.0 * j + 2.0).astype(BF16) for j in range(3)]
    swapped = [jnp.where(half16, 2.0 * j + 2.0, 2.0 * j + 1.0).astype(BF16) for j in range(3)]

    def expand(g):
        start = pl.multiple_of(g * 16, 16)

        @pl.loop(0, 24, step=4)
        def _(r0):
            val, val_r = [], []
            for u in range(4):
                val.append([dd[g, r0 + u, :, tile(j)] for j in range(3)])
                val_r.append([pltpu.roll(v.astype(F32), 64, 1).astype(BF16) for v in val[u]])
            for m in range(6):
                t = tm[pl.ds(start, 16), tile(m)]
                acc = [jnp.zeros((16, 128), BF16)] * 4
                for j in GROUPS[m]:
                    straight, crossed = t == plain[j], t == swapped[j]
                    for u in range(4):
                        acc[u] = jnp.where(straight, val[u][j], acc[u])
                        acc[u] = jnp.where(crossed, val_r[u][j], acc[u])
                for u in range(4):
                    at = pl.multiple_of((r0 + u) * 128 + g * 16, 16)
                    ee[pl.ds(at, 16), tile(m)] = acc[u]

    expand(c * 4 + a)

    for k in range(1, 8):
        v = (zl + k) % 8
        send(cp.at[v], cp.at[v], sp.at[k], rp.at[v], p, v).wait_recv()
    goal_p = [jnp.where(half24, 2.0 * j + 1.0, 2.0 * j + 2.0) for j in range(3)]
    goal_s = [jnp.where(half24, 2.0 * j + 2.0, 2.0 * j + 1.0) for j in range(3)]

    @pl.loop(0, 8)
    def _(q):
        val = [cp[q, :, tile(j)].astype(F32) for j in range(3)]
        val_r = [pltpu.roll(v, 64, 1) for v in val]
        for m in range(6):
            t = jnp.broadcast_to(tp[q, :, tile(m)], (24, 128))
            acc = jnp.zeros((24, 128), F32)
            for j in GROUPS[m]:
                acc = jnp.where(t == goal_p[j], val[j], acc)
                acc = jnp.where(t == goal_s[j], val_r[j], acc)
            mp[q, :, tile(m)] = acc

    for m in range(6):
        ft[m] = mp[:, :, tile(m)].reshape(192, 128).T.astype(BF16)

    other = y * (1 - c) + x * c

    def from_core(v):
        ref = dd.at[(1 - c) * 4 + v]
        send(ref, ref, sd.at[v], rd.at[v], core_peer, zl).wait_recv()
        expand((1 - c) * 4 + v)

    from_core(other)
    for k in (1, 3, 2):
        v = (a + k) % 4
        ref = dd.at[c * 4 + v]
        send(ref, ref, sc.at[k - 1], rc.at[v], at_a(k), zl).wait_recv()
        to_core(v).start()
        expand(c * 4 + v)
    for k in (1, 3, 2):
        from_core((other + k) % 4)

    @pl.loop(0, 3)
    def _(n):
        cols = pl.ds(pl.multiple_of(n * 256, 256), 256)
        got = jnp.dot(gt[...], ee[:, cols], preferred_element_type=F32)
        pt[:, :, cols] = got.reshape(8, 24, 256)

    def right(j):
        return send(rr.at[j], rr.at[j], s_r.at[j], r_r.at[j], p, (zl + 1) % 8)

    def left(j):
        return send(rl.at[j], rl.at[j], s_l.at[j], r_l.at[j], p, (zl + 7) % 8)

    def slot(s):
        @pl.when(zl <= s)
        def _():
            j = zl + 7 - s

            @pl.when(zl > 0)
            def _():
                right(j).wait_recv()
                rr[j] = rr[j] + pt[j]

            @pl.when(zl == 0)
            def _():
                rr[j] = pt[j]

            right(j).start()

        @pl.when(zl >= 7 - s)
        def _():
            j = zl - 7 + s

            @pl.when(zl < 7)
            def _():
                left(j).wait_recv()
                rl[j] = rl[j] + pt[j]

            @pl.when(zl == 7)
            def _():
                rl[j] = pt[j]

            left(j).start()

        if s >= 2:

            @pl.when(zl <= s - 2)
            def _():
                right(zl + 9 - s).wait_send()

            @pl.when(zl >= 9 - s)
            def _():
                left(zl - 9 + s).wait_send()

    slot(0)

    half128 = lax.broadcasted_iota(jnp.int32, (128, 128), 0) < 64
    for m in range(6):
        part = pt[:, :, tile(m)].reshape(192, 128)
        hi = part.astype(BF16)
        lo = (part - hi.astype(F32)).astype(BF16)
        both = jnp.dot(ft[m], hi, preferred_element_type=F32)
        both = both + jnp.dot(ft[m], lo, preferred_element_type=F32)
        both = jnp.where(half128, both, pltpu.roll(both, 64, 1)).T
        for v in range(8):
            sh[v * 3 + m // 2, :, tile(m % 2)] = both[v * 8 : v * 8 + 8]

    owner = d < 24

    def share_to(k):
        v = (d + k) % 24
        return send(sh.at[v], b1.at[d], s1.at[k], r1.at[d], in_plane(v), zl)

    def piece_to(k):
        return send(b6.at[d], b6.at[d], s6.at[k], r6.at[d], in_plane(d + k), zl)

    def to_line(k):
        return send(b3.at[zl], b3.at[zl], s3.at[k], r3.at[zl], p, (zl + k) % 8)

    def to_pair():
        peer = prow_of(x, zh + 1 - 2 * (zh % 2), y, c)
        return send(b4.at[0], b4.at[1], s4.at[0], r4.at[0], peer, zl)

    def to_other_pair():
        return send(b4.at[2], b4.at[3], s4.at[1], r4.at[1], prow_of(x, 3 - zh, y, c), zl)

    def total(ref, n):
        parts = [ref[v] for v in range(n)]
        while len(parts) > 1:
            parts = [u + v for u, v in zip(parts[::2], parts[1::2])]
        return parts[0]

    def phase1():
        @pl.when(d >= 24)
        def _():
            share_to(0).start()

        for k in range(1, 24):
            share_to(k).start()

    def phase2():
        @pl.when(owner)
        def _():
            b1[d] = sh[d]
            for k in range(1, 32):
                v = (d + k) % 32
                send(b1.at[v], b1.at[v], s1.at[0], r1.at[v], in_plane(v), zl).wait_recv()
            b3[zl] = total(b1, 32)
            for k in range(1, 8):
                to_line(k).start()

    def phase3():
        @pl.when(owner)
        def _():
            for k in range(1, 8):
                v = (zl + k) % 8
                send(b3.at[v], b3.at[v], s3.at[k], r3.at[v], p, v).wait_recv()
            b4[0] = total(b3, 8)
            to_pair().start()

    def phase3b():
        @pl.when(owner)
        def _():
            to_pair().wait_recv()
            b4[2] = b4[0] + b4[1]
            to_other_pair().start()

    def phase4():
        @pl.when(owner)
        def _():
            to_other_pair().wait_recv()
            b6[d] = b4[2] + b4[3]
            for k in range(1, 32):
                piece_to(k).start()

    def phase5():
        for v in range(24):

            @pl.when(d != v)
            def _():
                home = prow_of(v // 8, zh, (v // 2) % 4, v % 2)
                send(b6.at[v], b6.at[v], s6.at[0], r6.at[v], home, zl).wait_recv()

        for v in range(24):
            rows, cols = slice(v // 3 * 8, v // 3 * 8 + 8), slice(v % 3 * 256, v % 3 * 256 + 256)
            diag_ref[rows, cols] = dinv_ref[rows, cols] - b6[v]

    phase1()
    slot(1)
    slot(2)
    phase2()
    slot(3)
    slot(4)
    phase3()
    slot(5)
    phase3b()
    slot(6)

    off_ref[...] = pt[zl]

    @pl.when(zl > 0)
    def _():
        right(zl).wait_recv()
        off_ref[...] += rr[zl]

    @pl.when(zl < 7)
    def _():
        left(zl).wait_recv()
        off_ref[...] += rl[zl]

    phase4()
    phase5()

    for copy in to_zh:
        copy.wait_send()
    for v in range(4):
        for copy in forward(v):
            copy.wait_send()
    for copy in to_zl:
        copy.wait_send()
    for copy in to_a:
        copy.wait_send()
    for v in range(4):
        to_core(v).wait_send()
    for s in (5, 6):

        @pl.when(zl <= s)
        def _():
            right(zl + 7 - s).wait_send()

        @pl.when(zl >= 7 - s)
        def _():
            left(zl - 7 + s).wait_send()

    @pl.when(d >= 24)
    def _():
        share_to(0).wait_send()

    for k in range(1, 24):
        share_to(k).wait_send()

    @pl.when(owner)
    def _():
        for k in range(1, 8):
            to_line(k).wait_send()
        to_pair().wait_send()
        to_other_pair().wait_send()
        for k in range(1, 32):
            piece_to(k).wait_send()


def body(ainv_sep, lower_blocks, pattern, diag_inv):
    dma = pltpu.SemaphoreType.DMA
    vmem = pltpu.VMEM
    off, diag = pl.pallas_call(
        kernel,
        out_shape=(
            jax.ShapeDtypeStruct((24, 768), F32),
            jax.ShapeDtypeStruct((64, 768), F32),
        ),
        in_specs=[pl.BlockSpec(memory_space=pl.ANY)] * 4,
        out_specs=(pl.BlockSpec(memory_space=vmem), pl.BlockSpec(memory_space=vmem)),
        scratch_shapes=[
            vmem((12, 1024), jnp.int32),
            vmem((24, 768), BF16),
            vmem((64, 768), F32),
            vmem((16, 24, 384), BF16),
            vmem((8, 24, 16, 384), BF16),
            vmem((8, 24, 384), BF16),
            vmem((24, 192, 128), BF16),
            vmem((192, 3072), BF16),
            vmem((128, 768), BF16),
            vmem((8, 1, 768), F32),
            vmem((3072, 768), BF16),
            vmem((8, 24, 768), F32),
            vmem((6, 128, 192), BF16),
            vmem((8, 24, 768), F32),
            vmem((8, 24, 768), F32),
            vmem((8, 24, 768), F32),
            vmem((24, 8, 256), F32),
            vmem((32, 8, 256), F32),
            vmem((8, 8, 256), F32),
            vmem((4, 8, 256), F32),
            vmem((24, 8, 256), F32),
            dma((4,)),
            dma((3,)), dma((4,)),
            dma((4, 3)), dma((16,)),
            dma((3,)), dma((4,)),
            dma((4,)), dma((4,)),
            dma((8,)), dma((8,)),
            dma((8,)), dma((8,)),
            dma((8,)), dma((8,)),
            dma((24,)), dma((32,)),
            dma((8,)), dma((8,)),
            dma((2,)), dma((2,)),
            dma((32,)), dma((24,)),
        ],
        compiler_params=pltpu.CompilerParams(
            collective_id=0, has_side_effects=True, vmem_limit_bytes=60 * 1024 * 1024
        ),
    )(
        pattern.T,
        lower_blocks,
        diag_inv.T,
        ainv_sep.transpose(1, 2, 3, 0).reshape(24, 192, 128),
    )
    return off, diag.T


def solution(mesh):
    return jax.shard_map(
        body,
        mesh=mesh,
        in_specs=(P(None, "pcol", None, "prow"), P(("prow", "pcol"), None), P(), P()),
        out_specs=(P(("prow", "pcol"), None), P()),
        check_vma=False,
    )
```

```python
import functools

import jax
import jax.numpy as jnp
from jax import lax
from jax.experimental import pallas as pl
from jax.experimental.pallas import tpu as pltpu
from jax.sharding import PartitionSpec as P

MESH = pl.DeviceIdType.MESH
F32, BF16 = jnp.float32, jnp.bfloat16
GROUPS = [[j for j in range(3) if (j <= m if m < 3 else j >= m - 3)] for m in range(6)]


def tile(m):
    return slice(m * 128, (m + 1) * 128)


def prow_of(x, zh, y, c):
    return ((x * 4 + zh) * 4 + y) * 2 + c


def place(i):
    c, zh, a, w = i >> 6, (i >> 4) & 3, (i >> 2) & 3, i & 3
    x = jnp.where(c == 0, a, w)
    y = jnp.where(c == 0, w, a)
    return (x << 5) + (zh << 3) + (y << 1) + c


def slot_rows(pat):
    rows = [pat[k : k + 1, :] for k in range(12)]
    out = [None] * 12
    run = jnp.zeros_like(rows[0])
    for k in range(6):
        run = run + rows[k]
        out[k] = run * rows[k]
    run = jnp.full_like(rows[0], 6.0)
    for k in range(11, 5, -1):
        out[k] = run * rows[k]
        run = run - rows[k]
    return jnp.concatenate(out + [jnp.zeros_like(rows[0])] * 4, axis=0)


def kernel(
    pat_hbm, low_hbm, dinv_hbm, g_hbm, off_ref, diag_ref,
    pat_ref, low_ref, dinv_ref, cb, dd, cp, gv, gt, tm, tp, ee, mp, ft, pt, rr, rl, sh, b1, b3, b4, b6,
    isem, sa, ra, sb, rb, sc, rc, sd, rd, sp, rp, s_r, r_r, s_l, r_l,
    s1, r1, s3, r3, s4, r4, s6, r6,
):
    p = lax.axis_index("prow")
    zl = lax.axis_index("pcol")
    c, y, zh, x = p % 2, (p // 2) % 4, (p // 8) % 4, p // 32
    w = y * (1 - c) + x * c
    a = x * (1 - c) + y * c

    def send(src, dst, ssem, rsem, prow, pcol):
        return pltpu.make_async_remote_copy(
            src_ref=src, dst_ref=dst, send_sem=ssem, recv_sem=rsem,
            device_id=(prow, pcol), device_id_type=MESH,
        )

    def at_zh(k):
        return prow_of(x, (zh + k) % 4, y, c)

    def at_w(k):
        v = (w + k) % 4
        return prow_of(x * (1 - c) + v * c, zh, v * (1 - c) + y * c, c)

    def at_a(k):
        v = (a + k) % 4
        return prow_of(v * (1 - c) + x * c, zh, y * (1 - c) + v * c, c)

    core_peer = prow_of(x, zh, y, 1 - c)
    d = (x * 4 + y) * 2 + c

    def in_plane(v):
        return prow_of((v // 8) % 4, zh, (v // 2) % 4, v % 2)


    barrier = pltpu.get_barrier_semaphore()
    for k in (1, 3):
        pl.semaphore_signal(barrier, inc=1, device_id=(at_zh(k), zl), device_id_type=MESH)
    for k in range(1, 8):
        pl.semaphore_signal(barrier, inc=1, device_id=(p, (zl + k) % 8), device_id_type=MESH)
    for k in range(1, 32):
        pl.semaphore_signal(barrier, inc=1, device_id=(in_plane(d + k), zl), device_id_type=MESH)

    pairs = [(pat_hbm, pat_ref), (low_hbm, low_ref), (g_hbm, gv), (dinv_hbm, dinv_ref)]
    loads = [pltpu.make_async_copy(u, v, isem.at[k]) for k, (u, v) in enumerate(pairs)]
    for copy in loads:
        copy.start()
    loads[0].wait()
    loads[1].wait()

    slots = slot_rows(pat_ref[...].astype(F32)).astype(BF16)
    row = lax.broadcasted_iota(jnp.int32, (144, 128), 0)
    lane = lax.broadcasted_iota(jnp.int32, (144, 128), 1)
    wanted = jnp.where(row < 128, (place(row & 127) << 3) + zl, p * 8 + (row & 7)) - lane
    pick = [jnp.where(wanted == 128 * k, 1.0, 0.0).astype(BF16) for k in range(8)]
    pick = jnp.concatenate(pick, axis=1)
    table = lax.dot_general(pick, slots, (((1,), (1,)), ((), ())), preferred_element_type=F32)
    low_half = lane < 64
    for m in range(6):
        t = jnp.where(low_half, table[:, 2 * m : 2 * m + 1], table[:, 2 * m + 1 : 2 * m + 2])
        tm[:, tile(m)] = t[:128].astype(BF16)
        for q in range(8):
            tp[q, :, tile(m)] = t[128 + q : 129 + q]

    half24 = lax.broadcasted_iota(jnp.int32, (24, 128), 1) < 64
    own = cb.at[zh, a, w]
    mine = tp[zl]
    parts = [None] * 3
    for m in range(6):
        val = low_ref[:, tile(m)].astype(F32)
        t = jnp.broadcast_to(mine[:, tile(m)], (24, 128))
        val_r, t_r = pltpu.roll(val, 64, 1), pltpu.roll(t, 64, 1)
        for j in GROUPS[m]:
            goal = jnp.where(half24, 2.0 * j + 1.0, 2.0 * j + 2.0)
            got = jnp.where(t == goal, val, 0.0) + jnp.where(t_r == goal, val_r, 0.0)
            parts[j] = got if parts[j] is None else parts[j] + got
    for j in range(3):
        own[:, tile(j)] = parts[j].astype(BF16)
        cp[zl, :, tile(j)] = parts[j].astype(BF16)

    pl.semaphore_wait(barrier, 40)

    below, above, far = (zh + 3 - 2 * c) % 4, (zh + 1 + 2 * c) % 4, (zh + 2) % 4

    def along_w(v):
        ref = cb.at[v, a, w]
        return [send(ref, ref, sb.at[v, k - 1], rb.at[v, w], at_w(k), zl) for k in range(1, 4)]

    def got_w(v):
        for k in (1, 3, 2):
            u = (w + k) % 4
            ref = cb.at[v, a, u]
            send(ref, ref, sb.at[v, 0], rb.at[v, u], at_w(k), zl).wait_recv()

    def along_a(v):
        ref = cb.at[v, a]
        return [send(ref, ref, sc.at[v, k - 1], rc.at[v, a], at_a(k), zl) for k in range(1, 4)]

    def got_a(v):
        for k in (1, 3, 2):
            u = (a + k) % 4
            ref = cb.at[v, u]
            send(ref, ref, sc.at[v, 0], rc.at[v, u], at_a(k), zl).wait_recv()

    def to_core(v):
        ref = dd.at[c * 4 + v]
        return send(ref, ref, sd.at[v], rd.at[v], core_peer, zl)

    def handed_on():
        ref = cb.at[below, a, w]
        return send(ref, ref, sa.at[2], ra.at[below], at_zh(1 + 2 * c), zl)

    def got_zh(v):
        ref = cb.at[v, a, w]
        send(ref, ref, sa.at[0], ra.at[v], at_zh(1), zl).wait_recv()

    def begin(copies):
        for copy in copies:
            copy.start()

    to_zh = [send(own, own, sa.at[k // 2], ra.at[zh], at_zh(k), zl) for k in (1, 3)]
    begin(to_zh)
    begin(along_w(zh))

    gi = lax.broadcasted_iota(jnp.int32, (128, 128), 0)
    gj = lax.broadcasted_iota(jnp.int32, (128, 128), 1)
    perm = jnp.where(gi == place(gj), -1.0, 0.0).astype(BF16)
    oi = lax.broadcasted_iota(jnp.int32, (384, 128), 0)
    oj = lax.broadcasted_iota(jnp.int32, (384, 128), 1)
    source = (oi & 15) * 24 + (oi >> 4) - oj
    order = [jnp.where(source == 128 * k, 1.0, 0.0).astype(BF16) for k in range(3)]
    order = jnp.concatenate(order, axis=1)

    loads[2].wait()
    loads[3].wait()
    for r in range(24):
        gt[:, tile(r)] = jnp.dot(gv[r], perm, preferred_element_type=F32).astype(BF16)

    half16 = lax.broadcasted_iota(jnp.int32, (16, 128), 1) < 64
    plain = [jnp.where(half16, 2.0 * j + 1.0, 2.0 * j + 2.0).astype(BF16) for j in range(3)]
    swapped = [jnp.where(half16, 2.0 * j + 2.0, 2.0 * j + 1.0).astype(BF16) for j in range(3)]

    def expand(g):
        start = pl.multiple_of(g * 16, 16)

        @pl.loop(0, 24, step=4)
        def _(r0):
            val, val_r = [], []
            for u in range(4):
                val.append([dd[g, r0 + u, :, tile(j)] for j in range(3)])
                val_r.append([pltpu.roll(v.astype(F32), 64, 1).astype(BF16) for v in val[u]])
            for m in range(6):
                t = tm[pl.ds(start, 16), tile(m)]
                acc = [jnp.zeros((16, 128), BF16)] * 4
                for j in GROUPS[m]:
                    straight, crossed = t == plain[j], t == swapped[j]
                    for u in range(4):
                        acc[u] = jnp.where(straight, val[u][j], acc[u])
                        acc[u] = jnp.where(crossed, val_r[u][j], acc[u])
                for u in range(4):
                    at = pl.multiple_of((r0 + u) * 128 + g * 16, 16)
                    ee[pl.ds(at, 16), tile(m)] = acc[u]

    goal_p = [jnp.where(half24, 2.0 * j + 1.0, 2.0 * j + 2.0) for j in range(3)]
    goal_s = [jnp.where(half24, 2.0 * j + 2.0, 2.0 * j + 1.0) for j in range(3)]

    def line_rows():
        @pl.loop(0, 8)
        def _(q):
            val = [cp[q, :, tile(j)].astype(F32) for j in range(3)]
            val_r = [pltpu.roll(v, 64, 1) for v in val]
            for m in range(6):
                t = jnp.broadcast_to(tp[q, :, tile(m)], (24, 128))
                acc = jnp.zeros((24, 128), F32)
                for j in GROUPS[m]:
                    acc = jnp.where(t == goal_p[j], val[j], acc)
                    acc = jnp.where(t == goal_s[j], val_r[j], acc)
                mp[q, :, tile(m)] = acc

        for m in range(6):
            ft[m] = mp[:, :, tile(m)].reshape(192, 128).T.astype(BF16)

    def regroup(v):
        group = cb[v].astype(F32).reshape(384, 384).astype(BF16)
        group = jnp.dot(order, group, preferred_element_type=F32)
        dd[c * 4 + v] = group.reshape(24, 16, 384).astype(BF16)
        to_core(v).start()

    def from_core(v):
        ref = dd.at[(1 - c) * 4 + v]
        send(ref, ref, sd.at[v], rd.at[v], core_peer, zl).wait_recv()
        expand((1 - c) * 4 + v)

    to_zl = [
        send(cp.at[zl], cp.at[zl], sp.at[k], rp.at[zl], p, (zl + k) % 8) for k in range(1, 8)
    ]

    got_w(zh)
    begin(along_a(zh))
    got_zh(below)
    handed_on().start()
    begin(along_w(below))
    got_zh(above)
    begin(along_w(above))
    begin(to_zl)
    got_a(zh)
    regroup(zh)
    expand(c * 4 + zh)
    got_w(below)
    begin(along_a(below))
    got_w(above)
    begin(along_a(above))
    got_zh(far)
    begin(along_w(far))
    from_core(zh)
    got_a(below)
    regroup(below)
    got_a(above)
    regroup(above)
    got_w(far)
    begin(along_a(far))
    expand(c * 4 + below)
    expand(c * 4 + above)
    from_core(below)
    from_core(above)
    for k in range(1, 8):
        v = (zl + k) % 8
        send(cp.at[v], cp.at[v], sp.at[k], rp.at[v], p, v).wait_recv()
    line_rows()
    got_a(far)
    regroup(far)
    expand(c * 4 + far)
    from_core(far)

    @pl.loop(0, 3)
    def _(n):
        cols = pl.ds(pl.multiple_of(n * 256, 256), 256)
        got = jnp.dot(gt[...], ee[:, cols], preferred_element_type=F32)
        pt[:, :, cols] = got.reshape(8, 24, 256)

    def right(j):
        return send(rr.at[j], rr.at[j], s_r.at[j], r_r.at[j], p, (zl + 1) % 8)

    def left(j):
        return send(rl.at[j], rl.at[j], s_l.at[j], r_l.at[j], p, (zl + 7) % 8)

    def slot(s):
        @pl.when(zl <= s)
        def _():
            j = zl + 7 - s

            @pl.when(zl > 0)
            def _():
                right(j).wait_recv()
                rr[j] = rr[j] + pt[j]

            @pl.when(zl == 0)
            def _():
                rr[j] = pt[j]

            right(j).start()

        @pl.when(zl >= 7 - s)
        def _():
            j = zl - 7 + s

            @pl.when(zl < 7)
            def _():
                left(j).wait_recv()
                rl[j] = rl[j] + pt[j]

            @pl.when(zl == 7)
            def _():
                rl[j] = pt[j]

            left(j).start()

        if s >= 2:

            @pl.when(zl <= s - 2)
            def _():
                right(zl + 9 - s).wait_send()

            @pl.when(zl >= 9 - s)
            def _():
                left(zl - 9 + s).wait_send()

    slot(0)

    half128 = lax.broadcasted_iota(jnp.int32, (128, 128), 0) < 64
    for m in range(6):
        part = pt[:, :, tile(m)].reshape(192, 128)
        hi = part.astype(BF16)
        lo = (part - hi.astype(F32)).astype(BF16)
        both = jnp.dot(ft[m], hi, preferred_element_type=F32)
        both = both + jnp.dot(ft[m], lo, preferred_element_type=F32)
        both = jnp.where(half128, both, pltpu.roll(both, 64, 1)).T
        for v in range(8):
            sh[v * 3 + m // 2, :, tile(m % 2)] = both[v * 8 : v * 8 + 8]

    owner = d < 24

    def share_to(k):
        v = (d + k) % 24
        return send(sh.at[v], b1.at[d], s1.at[k], r1.at[d], in_plane(v), zl)

    def piece_to(k):
        return send(b6.at[d], b6.at[d], s6.at[k], r6.at[d], in_plane(d + k), zl)

    def to_line(k):
        return send(b3.at[zl], b3.at[zl], s3.at[k], r3.at[zl], p, (zl + k) % 8)

    def to_pair():
        peer = prow_of(x, zh + 1 - 2 * (zh % 2), y, c)
        return send(b4.at[0], b4.at[1], s4.at[0], r4.at[0], peer, zl)

    def to_other_pair():
        return send(b4.at[2], b4.at[3], s4.at[1], r4.at[1], prow_of(x, 3 - zh, y, c), zl)

    def total(ref, n):
        parts = [ref[v] for v in range(n)]
        while len(parts) > 1:
            parts = [u + v for u, v in zip(parts[::2], parts[1::2])]
        return parts[0]

    def phase1():
        @pl.when(d >= 24)
        def _():
            share_to(0).start()

        for k in range(1, 24):
            share_to(k).start()

    def phase2():
        @pl.when(owner)
        def _():
            b1[d] = sh[d]
            for k in range(1, 32):
                v = (d + k) % 32
                send(b1.at[v], b1.at[v], s1.at[0], r1.at[v], in_plane(v), zl).wait_recv()
            b3[zl] = total(b1, 32)
            for k in range(1, 8):
                to_line(k).start()

    def phase3():
        @pl.when(owner)
        def _():
            for k in range(1, 8):
                v = (zl + k) % 8
                send(b3.at[v], b3.at[v], s3.at[k], r3.at[v], p, v).wait_recv()
            b4[0] = total(b3, 8)
            to_pair().start()

    def phase3b():
        @pl.when(owner)
        def _():
            to_pair().wait_recv()
            b4[2] = b4[0] + b4[1]
            to_other_pair().start()

    def phase4():
        @pl.when(owner)
        def _():
            to_other_pair().wait_recv()
            b6[d] = b4[2] + b4[3]
            for k in range(1, 32):
                piece_to(k).start()

    def phase5():
        for v in range(24):

            @pl.when(d != v)
            def _():
                home = prow_of(v // 8, zh, (v // 2) % 4, v % 2)
                send(b6.at[v], b6.at[v], s6.at[0], r6.at[v], home, zl).wait_recv()

        for v in range(24):
            rows, cols = slice(v // 3 * 8, v // 3 * 8 + 8), slice(v % 3 * 256, v % 3 * 256 + 256)
            diag_ref[rows, cols] = dinv_ref[rows, cols] - b6[v]

    phase1()
    slot(1)
    slot(2)
    phase2()
    slot(3)
    slot(4)
    phase3()
    slot(5)
    phase3b()
    slot(6)

    off_ref[...] = pt[zl]

    @pl.when(zl > 0)
    def _():
        right(zl).wait_recv()
        off_ref[...] += rr[zl]

    @pl.when(zl < 7)
    def _():
        left(zl).wait_recv()
        off_ref[...] += rl[zl]

    phase4()
    phase5()

    for copy in to_zh + to_zl:
        copy.wait_send()
    handed_on().wait_send()
    for v in range(4):
        for copy in along_w(v) + along_a(v):
            copy.wait_send()
        to_core(v).wait_send()
    for s in (5, 6):

        @pl.when(zl <= s)
        def _():
            right(zl + 7 - s).wait_send()

        @pl.when(zl >= 7 - s)
        def _():
            left(zl - 7 + s).wait_send()

    @pl.when(d >= 24)
    def _():
        share_to(0).wait_send()

    for k in range(1, 24):
        share_to(k).wait_send()

    @pl.when(owner)
    def _():
        for k in range(1, 8):
            to_line(k).wait_send()
        to_pair().wait_send()
        to_other_pair().wait_send()
        for k in range(1, 32):
            piece_to(k).wait_send()


def body(ainv_sep, lower_blocks, pattern, diag_inv):
    dma = pltpu.SemaphoreType.DMA
    vmem = pltpu.VMEM
    off, diag = pl.pallas_call(
        kernel,
        out_shape=(
            jax.ShapeDtypeStruct((24, 768), F32),
            jax.ShapeDtypeStruct((64, 768), F32),
        ),
        in_specs=[pl.BlockSpec(memory_space=pl.ANY)] * 4,
        out_specs=(pl.BlockSpec(memory_space=vmem), pl.BlockSpec(memory_space=vmem)),
        scratch_shapes=[
            vmem((12, 1024), jnp.int32),
            vmem((24, 768), BF16),
            vmem((64, 768), F32),
            vmem((4, 4, 4, 24, 384), BF16),
            vmem((8, 24, 16, 384), BF16),
            vmem((8, 24, 384), BF16),
            vmem((24, 192, 128), BF16),
            vmem((192, 3072), BF16),
            vmem((128, 768), BF16),
            vmem((8, 1, 768), F32),
            vmem((3072, 768), BF16),
            vmem((8, 24, 768), F32),
            vmem((6, 128, 192), BF16),
            vmem((8, 24, 768), F32),
            vmem((8, 24, 768), F32),
            vmem((8, 24, 768), F32),
            vmem((24, 8, 256), F32),
            vmem((32, 8, 256), F32),
            vmem((8, 8, 256), F32),
            vmem((4, 8, 256), F32),
            vmem((24, 8, 256), F32),
            dma((4,)),
            dma((3,)), dma((4,)),
            dma((4, 3)), dma((4, 4)),
            dma((4, 3)), dma((4, 4)),
            dma((4,)), dma((4,)),
            dma((8,)), dma((8,)),
            dma((8,)), dma((8,)),
            dma((8,)), dma((8,)),
            dma((24,)), dma((32,)),
            dma((8,)), dma((8,)),
            dma((2,)), dma((2,)),
            dma((32,)), dma((24,)),
        ],
        compiler_params=pltpu.CompilerParams(
            collective_id=0, has_side_effects=True, vmem_limit_bytes=60 * 1024 * 1024
        ),
    )(
        pattern.T,
        lower_blocks,
        diag_inv.T,
        ainv_sep.transpose(1, 2, 3, 0).reshape(24, 192, 128),
    )
    return off, diag.T


def solution(mesh):
    return jax.shard_map(
        body,
        mesh=mesh,
        in_specs=(P(None, "pcol", None, "prow"), P(("prow", "pcol"), None), P(), P()),
        out_specs=(P(("prow", "pcol"), None), P()),
        check_vma=False,
    )
```

```python
import functools

import jax
import jax.numpy as jnp
from jax import lax
from jax.experimental import pallas as pl
from jax.experimental.pallas import tpu as pltpu
from jax.sharding import PartitionSpec as P

MESH = pl.DeviceIdType.MESH
F32, BF16 = jnp.float32, jnp.bfloat16
GROUPS = [[j for j in range(3) if (j <= m if m < 3 else j >= m - 3)] for m in range(6)]


def tile(m):
    return slice(m * 128, (m + 1) * 128)


def prow_of(x, zh, y, c):
    return ((x * 4 + zh) * 4 + y) * 2 + c


def place(i):
    c, zh, a, w = i >> 6, (i >> 4) & 3, (i >> 2) & 3, i & 3
    x = jnp.where(c == 0, a, w)
    y = jnp.where(c == 0, w, a)
    return (x << 5) + (zh << 3) + (y << 1) + c


def slot_rows(pat):
    rows = [pat[k : k + 1, :] for k in range(12)]
    out = [None] * 12
    run = jnp.zeros_like(rows[0])
    for k in range(6):
        run = run + rows[k]
        out[k] = run * rows[k]
    run = jnp.full_like(rows[0], 6.0)
    for k in range(11, 5, -1):
        out[k] = run * rows[k]
        run = run - rows[k]
    return jnp.concatenate(out + [jnp.zeros_like(rows[0])] * 4, axis=0)


def kernel(
    pat_hbm, low_hbm, dinv_hbm, g_hbm, off_ref, diag_ref,
    pat_ref, low_ref, dinv_ref, cb, dd, cp, gv, gt, tm, tp, ee, mp, ft, pt, rr, rl, sh, b1, b3, b4, b6,
    isem, sa, ra, sb, rb, sc, rc, sf, rf, sd, rd, sp, rp, s_r, r_r, s_l, r_l,
    s1, r1, s3, r3, s4, r4, s6, r6,
):
    p = lax.axis_index("prow")
    zl = lax.axis_index("pcol")
    c, y, zh, x = p % 2, (p // 2) % 4, (p // 8) % 4, p // 32
    w = y * (1 - c) + x * c
    a = x * (1 - c) + y * c

    def send(src, dst, ssem, rsem, prow, pcol):
        return pltpu.make_async_remote_copy(
            src_ref=src, dst_ref=dst, send_sem=ssem, recv_sem=rsem,
            device_id=(prow, pcol), device_id_type=MESH,
        )

    def at_zh(k):
        return prow_of(x, (zh + k) % 4, y, c)

    def at_w(k):
        v = (w + k) % 4
        return prow_of(x * (1 - c) + v * c, zh, v * (1 - c) + y * c, c)

    def at_a(k):
        v = (a + k) % 4
        return prow_of(v * (1 - c) + x * c, zh, y * (1 - c) + v * c, c)

    core_peer = prow_of(x, zh, y, 1 - c)
    d = (x * 4 + y) * 2 + c

    def in_plane(v):
        return prow_of((v // 8) % 4, zh, (v // 2) % 4, v % 2)


    barrier = pltpu.get_barrier_semaphore()
    for k in (1, 3):
        pl.semaphore_signal(barrier, inc=1, device_id=(at_zh(k), zl), device_id_type=MESH)
    for k in range(1, 8):
        pl.semaphore_signal(barrier, inc=1, device_id=(p, (zl + k) % 8), device_id_type=MESH)
    for k in range(1, 32):
        pl.semaphore_signal(barrier, inc=1, device_id=(in_plane(d + k), zl), device_id_type=MESH)

    pairs = [(pat_hbm, pat_ref), (low_hbm, low_ref), (g_hbm, gv), (dinv_hbm, dinv_ref)]
    loads = [pltpu.make_async_copy(u, v, isem.at[k]) for k, (u, v) in enumerate(pairs)]
    for copy in loads:
        copy.start()
    loads[0].wait()
    loads[1].wait()

    slots = slot_rows(pat_ref[...].astype(F32)).astype(BF16)
    def slots_of(rows, wanted):
        lane = lax.broadcasted_iota(jnp.int32, (rows, 128), 1)
        pick = [jnp.where(wanted - lane == 128 * k, 1.0, 0.0).astype(BF16) for k in range(8)]
        table = lax.dot_general(
            jnp.concatenate(pick, axis=1), slots, (((1,), (1,)), ((), ())), preferred_element_type=F32
        )
        return [
            jnp.where(lane < 64, table[:, 2 * m : 2 * m + 1], table[:, 2 * m + 1 : 2 * m + 2])
            for m in range(6)
        ]

    for m, t in enumerate(slots_of(8, p * 8 + lax.broadcasted_iota(jnp.int32, (8, 128), 0))):
        for q in range(8):
            tp[q, :, tile(m)] = t[q : q + 1]

    half24 = lax.broadcasted_iota(jnp.int32, (24, 128), 1) < 64
    own = cb.at[zh, a, w]
    mine = tp[zl]
    parts = [None] * 3
    for m in range(6):
        val = low_ref[:, tile(m)].astype(F32)
        t = jnp.broadcast_to(mine[:, tile(m)], (24, 128))
        val_r, t_r = pltpu.roll(val, 64, 1), pltpu.roll(t, 64, 1)
        for j in GROUPS[m]:
            goal = jnp.where(half24, 2.0 * j + 1.0, 2.0 * j + 2.0)
            got = jnp.where(t == goal, val, 0.0) + jnp.where(t_r == goal, val_r, 0.0)
            parts[j] = got if parts[j] is None else parts[j] + got
    for j in range(3):
        own[:, tile(j)] = parts[j].astype(BF16)
        cp[zl, :, tile(j)] = parts[j].astype(BF16)

    pl.semaphore_wait(barrier, 40)

    below, above, far = (zh + 3 - 2 * c) % 4, (zh + 1 + 2 * c) % 4, (zh + 2) % 4

    def along_w(v):
        ref = cb.at[v, a, w]
        return [send(ref, ref, sb.at[v, k - 1], rb.at[v, w], at_w(k), zl) for k in range(1, 4)]

    def got_w(v):
        for k in (1, 3, 2):
            u = (w + k) % 4
            ref = cb.at[v, a, u]
            send(ref, ref, sb.at[v, 0], rb.at[v, u], at_w(k), zl).wait_recv()

    def along_a(v):
        ref = cb.at[v, a]
        return [send(ref, ref, sc.at[v, k - 1], rc.at[v, a], at_a(k), zl) for k in range(1, 4)]

    def got_a(v):
        for k in (1, 3, 2):
            u = (a + k) % 4
            ref = cb.at[v, u]
            send(ref, ref, sc.at[v, 0], rc.at[v, u], at_a(k), zl).wait_recv()

    def plane_at(ka, kw):
        u, v = (a + ka) % 4, (w + kw) % 4
        return prow_of(u * (1 - c) + v * c, zh, v * (1 - c) + u * c, c)

    others = [(ka, kw) for ka in (0, 1, 3, 2) for kw in (0, 1, 3, 2)][1:]

    def spread(v):
        ref = cb.at[v, a, w]
        return [
            send(ref, ref, sf.at[ka, kw], rf.at[a, w], plane_at(ka, kw), zl) for ka, kw in others
        ]

    def got_spread(v):
        for ka, kw in others:
            u, t = (a + ka) % 4, (w + kw) % 4
            ref = cb.at[v, u, t]
            send(ref, ref, sf.at[ka, kw], rf.at[u, t], plane_at(ka, kw), zl).wait_recv()

    def to_core(v):
        ref = dd.at[c * 4 + v]
        return send(ref, ref, sd.at[v], rd.at[v], core_peer, zl)

    def handed_on():
        ref = cb.at[below, a, w]
        return send(ref, ref, sa.at[2], ra.at[below], at_zh(1 + 2 * c), zl)

    def got_zh(v):
        ref = cb.at[v, a, w]
        send(ref, ref, sa.at[0], ra.at[v], at_zh(1), zl).wait_recv()

    def begin(copies):
        for copy in copies:
            copy.start()

    to_zh = [send(own, own, sa.at[k // 2], ra.at[zh], at_zh(k), zl) for k in (1, 3)]
    begin(to_zh)
    begin(along_w(zh))

    half16 = lax.broadcasted_iota(jnp.int32, (16, 128), 1) < 64
    plain = [jnp.where(half16, 2.0 * j + 1.0, 2.0 * j + 2.0).astype(BF16) for j in range(3)]
    swapped = [jnp.where(half16, 2.0 * j + 2.0, 2.0 * j + 1.0).astype(BF16) for j in range(3)]

    def expand(g):
        start = pl.multiple_of(g * 16, 16)

        @pl.loop(0, 24, step=4)
        def _(r0):
            val, val_r = [], []
            for u in range(4):
                val.append([dd[g, r0 + u, :, tile(j)] for j in range(3)])
                val_r.append([pltpu.roll(v.astype(F32), 64, 1).astype(BF16) for v in val[u]])
            for m in range(6):
                t = tm[pl.ds(start, 16), tile(m)]
                acc = [jnp.zeros((16, 128), BF16)] * 4
                for j in GROUPS[m]:
                    straight, crossed = t == plain[j], t == swapped[j]
                    for u in range(4):
                        acc[u] = jnp.where(straight, val[u][j], acc[u])
                        acc[u] = jnp.where(crossed, val_r[u][j], acc[u])
                for u in range(4):
                    at = pl.multiple_of((r0 + u) * 128 + g * 16, 16)
                    ee[pl.ds(at, 16), tile(m)] = acc[u]

    goal_p = [jnp.where(half24, 2.0 * j + 1.0, 2.0 * j + 2.0) for j in range(3)]
    goal_s = [jnp.where(half24, 2.0 * j + 2.0, 2.0 * j + 1.0) for j in range(3)]

    def line_rows():
        @pl.loop(0, 8)
        def _(q):
            val = [cp[q, :, tile(j)].astype(F32) for j in range(3)]
            val_r = [pltpu.roll(v, 64, 1) for v in val]
            for m in range(6):
                t = jnp.broadcast_to(tp[q, :, tile(m)], (24, 128))
                acc = jnp.zeros((24, 128), F32)
                for j in GROUPS[m]:
                    acc = jnp.where(t == goal_p[j], val[j], acc)
                    acc = jnp.where(t == goal_s[j], val_r[j], acc)
                mp[q, :, tile(m)] = acc

        for m in range(6):
            ft[m] = mp[:, :, tile(m)].reshape(192, 128).T.astype(BF16)

    def regroup(v):
        group = cb[v].astype(F32).reshape(384, 384).astype(BF16)
        group = jnp.dot(order, group, preferred_element_type=F32)
        dd[c * 4 + v] = group.reshape(24, 16, 384).astype(BF16)
        to_core(v).start()

    def from_core(v):
        ref = dd.at[(1 - c) * 4 + v]
        send(ref, ref, sd.at[v], rd.at[v], core_peer, zl).wait_recv()
        expand((1 - c) * 4 + v)

    to_zl = [
        send(cp.at[zl], cp.at[zl], sp.at[k], rp.at[zl], p, (zl + k) % 8) for k in range(1, 8)
    ]

    got_w(zh)
    begin(along_a(zh))
    got_zh(below)
    handed_on().start()
    begin(along_w(below))
    got_zh(above)
    begin(along_w(above))
    begin(to_zl)
    row = lax.broadcasted_iota(jnp.int32, (128, 128), 0)
    for m, t in enumerate(slots_of(128, (place(row) << 3) + zl)):
        tm[:, tile(m)] = t.astype(BF16)
    gi = lax.broadcasted_iota(jnp.int32, (128, 128), 0)
    gj = lax.broadcasted_iota(jnp.int32, (128, 128), 1)
    perm = jnp.where(gi == place(gj), -1.0, 0.0).astype(BF16)
    oi = lax.broadcasted_iota(jnp.int32, (384, 128), 0)
    oj = lax.broadcasted_iota(jnp.int32, (384, 128), 1)
    source = (oi & 15) * 24 + (oi >> 4) - oj
    order = [jnp.where(source == 128 * k, 1.0, 0.0).astype(BF16) for k in range(3)]
    order = jnp.concatenate(order, axis=1)

    loads[2].wait()
    loads[3].wait()
    for r in range(24):
        gt[:, tile(r)] = jnp.dot(gv[r], perm, preferred_element_type=F32).astype(BF16)

    got_a(zh)
    regroup(zh)
    expand(c * 4 + zh)
    got_w(below)
    begin(along_a(below))
    got_w(above)
    begin(along_a(above))
    got_zh(far)
    begin(spread(far))
    from_core(zh)
    got_a(below)
    regroup(below)
    got_a(above)
    regroup(above)
    expand(c * 4 + below)
    expand(c * 4 + above)
    from_core(below)
    from_core(above)
    got_spread(far)
    regroup(far)
    expand(c * 4 + far)
    from_core(far)

    @pl.loop(0, 3)
    def _(n):
        cols = pl.ds(pl.multiple_of(n * 256, 256), 256)
        got = jnp.dot(gt[...], ee[:, cols], preferred_element_type=F32)
        pt[:, :, cols] = got.reshape(8, 24, 256)

    def right(j):
        return send(rr.at[j], rr.at[j], s_r.at[j], r_r.at[j], p, (zl + 1) % 8)

    def left(j):
        return send(rl.at[j], rl.at[j], s_l.at[j], r_l.at[j], p, (zl + 7) % 8)

    def slot(s):
        @pl.when(zl <= s)
        def _():
            j = zl + 7 - s

            @pl.when(zl > 0)
            def _():
                right(j).wait_recv()
                rr[j] = rr[j] + pt[j]

            @pl.when(zl == 0)
            def _():
                rr[j] = pt[j]

            right(j).start()

        @pl.when(zl >= 7 - s)
        def _():
            j = zl - 7 + s

            @pl.when(zl < 7)
            def _():
                left(j).wait_recv()
                rl[j] = rl[j] + pt[j]

            @pl.when(zl == 7)
            def _():
                rl[j] = pt[j]

            left(j).start()

        if s >= 2:

            @pl.when(zl <= s - 2)
            def _():
                right(zl + 9 - s).wait_send()

            @pl.when(zl >= 9 - s)
            def _():
                left(zl - 9 + s).wait_send()

    slot(0)
    for k in range(1, 8):
        v = (zl + k) % 8
        send(cp.at[v], cp.at[v], sp.at[k], rp.at[v], p, v).wait_recv()
    line_rows()

    half128 = lax.broadcasted_iota(jnp.int32, (128, 128), 0) < 64
    for m in range(6):
        part = pt[:, :, tile(m)].reshape(192, 128)
        hi = part.astype(BF16)
        lo = (part - hi.astype(F32)).astype(BF16)
        both = jnp.dot(ft[m], hi, preferred_element_type=F32)
        both = both + jnp.dot(ft[m], lo, preferred_element_type=F32)
        both = jnp.where(half128, both, pltpu.roll(both, 64, 1)).T
        for v in range(8):
            sh[v * 3 + m // 2, :, tile(m % 2)] = both[v * 8 : v * 8 + 8]

    owner = d < 24

    def share_to(k):
        v = (d + k) % 24
        return send(sh.at[v], b1.at[d], s1.at[k], r1.at[d], in_plane(v), zl)

    def piece_to(k):
        return send(b6.at[d], b6.at[d], s6.at[k], r6.at[d], in_plane(d + k), zl)

    def to_line(k):
        return send(b3.at[zl], b3.at[zl], s3.at[k], r3.at[zl], p, (zl + k) % 8)

    def to_pair():
        peer = prow_of(x, zh + 1 - 2 * (zh % 2), y, c)
        return send(b4.at[0], b4.at[1], s4.at[0], r4.at[0], peer, zl)

    def to_other_pair():
        return send(b4.at[2], b4.at[3], s4.at[1], r4.at[1], prow_of(x, 3 - zh, y, c), zl)

    def total(ref, n):
        parts = [ref[v] for v in range(n)]
        while len(parts) > 1:
            parts = [u + v for u, v in zip(parts[::2], parts[1::2])]
        return parts[0]

    def phase1():
        @pl.when(d >= 24)
        def _():
            share_to(0).start()

        for k in range(1, 24):
            share_to(k).start()

    def phase2():
        @pl.when(owner)
        def _():
            b1[d] = sh[d]
            for k in range(1, 32):
                v = (d + k) % 32
                send(b1.at[v], b1.at[v], s1.at[0], r1.at[v], in_plane(v), zl).wait_recv()
            b3[zl] = total(b1, 32)
            for k in range(1, 8):
                to_line(k).start()

    def phase3():
        @pl.when(owner)
        def _():
            for k in range(1, 8):
                v = (zl + k) % 8
                send(b3.at[v], b3.at[v], s3.at[k], r3.at[v], p, v).wait_recv()
            b4[0] = total(b3, 8)
            to_pair().start()

    def phase3b():
        @pl.when(owner)
        def _():
            to_pair().wait_recv()
            b4[2] = b4[0] + b4[1]
            to_other_pair().start()

    def phase4():
        @pl.when(owner)
        def _():
            to_other_pair().wait_recv()
            b6[d] = b4[2] + b4[3]
            for k in range(1, 32):
                piece_to(k).start()

    def phase5():
        for v in range(24):

            @pl.when(d != v)
            def _():
                home = prow_of(v // 8, zh, (v // 2) % 4, v % 2)
                send(b6.at[v], b6.at[v], s6.at[0], r6.at[v], home, zl).wait_recv()

        for v in range(24):
            rows, cols = slice(v // 3 * 8, v // 3 * 8 + 8), slice(v % 3 * 256, v % 3 * 256 + 256)
            diag_ref[rows, cols] = dinv_ref[rows, cols] - b6[v]

    phase1()
    slot(1)
    slot(2)
    phase2()
    slot(3)
    slot(4)
    phase3()
    slot(5)
    phase3b()
    slot(6)

    off_ref[...] = pt[zl]

    @pl.when(zl > 0)
    def _():
        right(zl).wait_recv()
        off_ref[...] += rr[zl]

    @pl.when(zl < 7)
    def _():
        left(zl).wait_recv()
        off_ref[...] += rl[zl]

    phase4()
    phase5()

    for copy in to_zh + to_zl:
        copy.wait_send()
    handed_on().wait_send()
    for v in (zh, below, above):
        for copy in along_w(v) + along_a(v):
            copy.wait_send()
    for copy in spread(far):
        copy.wait_send()
    for v in range(4):
        to_core(v).wait_send()
    for s in (5, 6):

        @pl.when(zl <= s)
        def _():
            right(zl + 7 - s).wait_send()

        @pl.when(zl >= 7 - s)
        def _():
            left(zl - 7 + s).wait_send()

    @pl.when(d >= 24)
    def _():
        share_to(0).wait_send()

    for k in range(1, 24):
        share_to(k).wait_send()

    @pl.when(owner)
    def _():
        for k in range(1, 8):
            to_line(k).wait_send()
        to_pair().wait_send()
        to_other_pair().wait_send()
        for k in range(1, 32):
            piece_to(k).wait_send()


def body(ainv_sep, lower_blocks, pattern, diag_inv):
    dma = pltpu.SemaphoreType.DMA
    vmem = pltpu.VMEM
    off, diag = pl.pallas_call(
        kernel,
        out_shape=(
            jax.ShapeDtypeStruct((24, 768), F32),
            jax.ShapeDtypeStruct((64, 768), F32),
        ),
        in_specs=[pl.BlockSpec(memory_space=pl.ANY)] * 4,
        out_specs=(pl.BlockSpec(memory_space=vmem), pl.BlockSpec(memory_space=vmem)),
        scratch_shapes=[
            vmem((12, 1024), jnp.int32),
            vmem((24, 768), BF16),
            vmem((64, 768), F32),
            vmem((4, 4, 4, 24, 384), BF16),
            vmem((8, 24, 16, 384), BF16),
            vmem((8, 24, 384), BF16),
            vmem((24, 192, 128), BF16),
            vmem((192, 3072), BF16),
            vmem((128, 768), BF16),
            vmem((8, 1, 768), F32),
            vmem((3072, 768), BF16),
            vmem((8, 24, 768), F32),
            vmem((6, 128, 192), BF16),
            vmem((8, 24, 768), F32),
            vmem((8, 24, 768), F32),
            vmem((8, 24, 768), F32),
            vmem((24, 8, 256), F32),
            vmem((32, 8, 256), F32),
            vmem((8, 8, 256), F32),
            vmem((4, 8, 256), F32),
            vmem((24, 8, 256), F32),
            dma((4,)),
            dma((3,)), dma((4,)),
            dma((4, 3)), dma((4, 4)),
            dma((4, 3)), dma((4, 4)),
            dma((4, 4)), dma((4, 4)),
            dma((4,)), dma((4,)),
            dma((8,)), dma((8,)),
            dma((8,)), dma((8,)),
            dma((8,)), dma((8,)),
            dma((24,)), dma((32,)),
            dma((8,)), dma((8,)),
            dma((2,)), dma((2,)),
            dma((32,)), dma((24,)),
        ],
        compiler_params=pltpu.CompilerParams(
            collective_id=0, has_side_effects=True, vmem_limit_bytes=60 * 1024 * 1024
        ),
    )(
        pattern.T,
        lower_blocks,
        diag_inv.T,
        ainv_sep.transpose(1, 2, 3, 0).reshape(24, 192, 128),
    )
    return off, diag.T


def solution(mesh):
    return jax.shard_map(
        body,
        mesh=mesh,
        in_specs=(P(None, "pcol", None, "prow"), P(("prow", "pcol"), None), P(), P()),
        out_specs=(P(("prow", "pcol"), None), P()),
        check_vma=False,
    )
```
